512 devices in a mesh: dp: 32 (over x, z_lo, core), section: 8 (over y), mp: 2 (over z_hi).
Axes of the slice: x: 4, y: 8, z: 8 (z_hi: 2, z_lo: 4; z = z_hi * 4 + z_lo), core: 2. Of those that a mesh axis runs over, the one named last changes fastest.
Arguments:
- queries: bfloat16 [8, 4096, 2048], P('section', 'dp', 'mp'), may hold values from -45 to 45
- keys: bfloat16 [8, 8192, 2048], P('section', 'dp', 'mp'), may hold values from -6 to 6
- values: bfloat16 [8, 8192, 2048], P('section', 'dp', 'mp'), may hold values from -6 to 6
- out_grad: bfloat16 [8, 4096, 2048], P('section', 'dp', 'mp'), may hold values from -96 to 96
- key_weight: bfloat16 [8, 2048, 2048], P('section', 'dp', 'mp'), may hold values from -0.125 to 0.125
- encoded: bfloat16 [8192, 2048], P('dp', ('section', 'mp')), may hold values from -6 to 6
- enc_lengths: int32 [32], P('dp'), may hold values from 128 to 256
Outputs:
- query_grad: bfloat16 [8, 4096, 2048], P('section', 'dp', 'mp')
- encoder_grad: bfloat16 [8192, 2048], P('dp', ('section', 'mp'))
- weight_grad: float32 [8, 2048, 2048], P('section', 'dp', 'mp')
The draws below stay inside these ranges and needn't reach their ends.
All inputs are finite; a program needn't handle non-finite values.
Results may differ from the reference program's by a relative error of at most 0.0058.
Values may be sent and summed in bfloat16 or wider, within the bound.
A program may use at most 64 MiB of HBM per device.

```python
import jax
import jax.numpy as jnp
from jax import lax

D = 2048
HEADS = 8
HD = 256
ENC_LEN = 256
DEC_LEN = 128
SEQS = 32
LAYERS = 8
TOKENS_E = 8192
TOKENS_D = 4096


def draw_keys(key, part):
    key = jax.random.fold_in(key, 11)
    shape = (LAYERS, SEQS, ENC_LEN, HEADS * HD)
    base = jnp.clip(jax.random.normal(key, shape, jnp.float32), -6.0, 6.0)
    return base.reshape(LAYERS, SEQS * ENC_LEN, HEADS * HD).astype(jnp.bfloat16)


def draw_queries(key, part):
    key = jax.random.fold_in(key, 13)
    shape = (LAYERS, SEQS, DEC_LEN, HEADS * HD)
    base = jnp.clip(jax.random.normal(key, shape, jnp.float32), -6.0, 6.0)
    return base.reshape(LAYERS, SEQS * DEC_LEN, HEADS * HD).astype(jnp.bfloat16)


def plant(array, rng, smallest, high):
    place = [jax.random.randint(jax.random.fold_in(rng, axis), (), 0, length) for axis, length in enumerate(array.shape)]
    longest = array.shape.index(max(array.shape))
    next_to = place[:longest] + [(place[longest] + 1) % array.shape[longest]] + place[longest + 1:]
    return array.at[tuple(place)].set(smallest).at[tuple(next_to)].set(high)


def raised(array, stream_key, source, target, shards_of, factor):
    owner, partner = [(jnp.arange(array.shape[dim]) // (array.shape[dim] // shards_of)).reshape([-1 if axis == dim else 1 for axis in range(array.ndim)]) for dim in (source, target)]
    chosen = jax.random.permutation(stream_key, shards_of)[partner]
    strong = (owner == chosen) | (owner == (partner + shards_of // 2) % shards_of)
    return jnp.where(strong, factor * array, array)


def block_levels(own_key, shape, cuts, least, high):
    def one(dim, shards_of):
        draws = jax.random.uniform(jax.random.fold_in(jax.random.fold_in(own_key, 6), dim), (shards_of,), jnp.float32, least / len(cuts), high / len(cuts))
        return jnp.repeat(jnp.exp(draws), shape[dim] // shards_of).reshape((-1,) + (1,) * (len(shape) - dim - 1))

    gain = one(*cuts[0])
    for cut in cuts[1:]:
        gain = gain * one(*cut)
    return gain


def scatter_about(stream_key, shape, spread, reach, shards=(), held_as=jnp.bfloat16):
    values = spread * jax.random.normal(stream_key, shape, jnp.float32)
    if shards:
        values = values * block_levels(stream_key, shape, shards, -0.22, 0.18)
    return jnp.clip(values, -reach, reach).astype(held_as)


def noise_with(stream_key, dims, deviation, reach, split, heavy, kind=jnp.bfloat16):
    drawn = deviation * jax.random.normal(stream_key, dims, jnp.float32)
    if split:
        drawn = drawn * block_levels(stream_key, dims, split, -0.22, 0.18)
    return jnp.clip(raised(drawn, jax.random.fold_in(stream_key, 3), *heavy), -reach, reach).astype(kind)


def setup_inputs(seed: int = 0) -> dict:
    key_list = jax.random.split(jax.random.key(seed), 8)
    queries = draw_queries(jax.random.fold_in(key_list[7], 71), 0)
    keys = draw_keys(jax.random.fold_in(key_list[7], 71), 0)
    values = scatter_about(key_list[2], (LAYERS, TOKENS_E, HEADS * HD), 1.0, 6.0, ((0, 8), (1, 32), (2, 2)))
    out_grad = scatter_about(key_list[3], (LAYERS, TOKENS_D, HEADS * HD), 16.0, 96.0, ((0, 8), (1, 32), (2, 2)))
    key_weight = scatter_about(key_list[4], (LAYERS, D, HEADS * HD), D ** -0.5, 0.125, ((0, 8), (1, 32), (2, 2)))
    encoded = noise_with(key_list[5], (TOKENS_E, D), 1.0, 6.0, ((0, 32), (1, 16)), (0, 1, 32, 2.75))
    enc_lengths = plant(jax.random.randint(key_list[6], (SEQS,), ENC_LEN // 2, ENC_LEN + 1), jax.random.fold_in(key_list[6], 1), ENC_LEN // 2, ENC_LEN).astype(jnp.int32)
    return dict(queries=queries, keys=keys, values=values, out_grad=out_grad, key_weight=key_weight, encoded=encoded, enc_lengths=enc_lengths)


NEG_FILL = -1.0e30


def sequence_back(q, k, v, dout, length):
    scale = HD ** -0.5
    q_heads = q.reshape(DEC_LEN, HEADS, HD).astype(jnp.float32)
    k_heads = k.reshape(ENC_LEN, HEADS, HD).astype(jnp.float32)
    v_heads = v.reshape(ENC_LEN, HEADS, HD).astype(jnp.float32)
    d_heads = dout.reshape(DEC_LEN, HEADS, HD).astype(jnp.float32)
    scores = jnp.einsum("qhd,khd->hqk", q_heads, k_heads) * scale
    valid = jnp.arange(ENC_LEN) < length
    scores = jnp.where(valid[None, None, :], scores, NEG_FILL)
    top = jnp.max(scores, axis=-1, keepdims=True)
    expo = jnp.exp(scores - top)
    probs = expo / jnp.sum(expo, axis=-1, keepdims=True)
    dprobs = jnp.einsum("qhd,khd->hqk", d_heads, v_heads)
    delta = jnp.sum(probs * dprobs, axis=-1, keepdims=True)
    dscore = lax.optimization_barrier((probs * (dprobs - delta) * scale).astype(jnp.bfloat16)).astype(jnp.float32)
    query_part = jnp.einsum("hqk,khd->qhd", dscore, k_heads).astype(jnp.bfloat16)
    key_part = jnp.einsum("hqk,qhd->khd", dscore, q_heads).astype(jnp.bfloat16)
    return query_part.reshape(DEC_LEN, HEADS * HD), key_part.reshape(ENC_LEN, HEADS * HD)


def reference(queries, keys, values, out_grad, key_weight, encoded, enc_lengths):
    inner = HEADS * HD
    enc_seq = encoded.reshape(SEQS, ENC_LEN, D)

    def layer_back(total, items):
        q, k, v, dout, weight = items
        query_part, key_part = lax.map(
            lambda group: sequence_back(*group),
            (q.reshape(SEQS, DEC_LEN, inner), k.reshape(SEQS, ENC_LEN, inner),
             v.reshape(SEQS, ENC_LEN, inner), dout.reshape(SEQS, DEC_LEN, inner), enc_lengths))
        total = total + jnp.dot(key_part.reshape(TOKENS_E, inner), weight.T, preferred_element_type=jnp.float32)

        def add_bucket(acc, pair):
            rows, grads = pair
            term = jnp.dot(rows.T, grads, preferred_element_type=jnp.float32).astype(jnp.bfloat16)
            return acc + lax.optimization_barrier(term).astype(jnp.float32), None

        summed, _ = lax.scan(add_bucket, jnp.zeros((D, inner), jnp.float32), (enc_seq, key_part))
        return total, (query_part.reshape(TOKENS_D, inner), summed * (1.0 / SEQS))

    start = jnp.zeros((TOKENS_E, D), jnp.float32)
    total, (query_grad, weight_grad) = lax.scan(layer_back, start, (queries, keys, values, out_grad, key_weight))
    return query_grad, total.astype(jnp.bfloat16), weight_grad
```

```python
import jax
import jax.numpy as jnp
from jax import lax
from jax.experimental import pallas as pl
from jax.experimental.pallas import tpu as pltpu
from jax.sharding import PartitionSpec as P

HD = 256
NEG_FILL = -1e30
X, Z, Y = 4, 4, 8
F = X * Z
MESH = pl.DeviceIdType.MESH
BF = jnp.bfloat16
F32 = jnp.float32

NT = (((1,), (1,)), ((), ()))
NN = (((1,), (0,)), ((), ()))
TN = (((0,), (0,)), ((), ()))


def dot(a, b, dims):
    return lax.dot_general(a, b, dims, preferred_element_type=F32)


def kernel(
    q_hbm, k_hbm, v_hbm, d_hbm, w_hbm, enc_hbm, len_ref,
    qg_ref, eg_ref, wg_ref,
    q_v, k_v, v_v, d_v, enc_v, et, ebuf, wbuf, kg,
    term, e_send, e_recv, e_last, fin, enc_sum,
    part, a_send, a_recv, b_send, b_recv, z_send, z_recv,
    loc_sem, ws_sem, wr_sem, es_sem, er_sem, ks_sem, kr_sem,
    ts_sem, tr_sem, ls_sem, lr_sem, as_sem, ar_sem, bs_sem, br_sem, zs_sem, zr_sem,
):
    dp = lax.axis_index("dp")
    y = lax.axis_index("section")
    m = lax.axis_index("mp")
    x = dp // 8
    z = (dp // 2) % 4
    c = dp % 2
    f = dp // 2
    g = y * 2 + m

    def dev(x=x, z=z, c=c, y=y, m=m):
        return {"dp": x * 8 + z * 2 + c, "section": y, "mp": m}

    x_up, x_down = (x + 1) % X, (x + X - 1) % X
    y_up, y_down = (y + 1) % Y, (y + Y - 1) % Y
    sister, m_other = 1 - c, 1 - m
    dev_xu, dev_xd = dev(x=x_up), dev(x=x_down)
    dev_yu, dev_yd = dev(y=y_up), dev(y=y_down)
    dev_z = [None] + [dev(z=(z + dz) % Z) for dz in range(1, Z)]
    dev_s, dev_m, dev_ms = dev(c=sister), dev(m=m_other), dev(c=sister, m=m_other)

    partners = [dev_xu, dev_xd, dev_yu, dev_yd] + dev_z[1:] + [dev_s, dev_m, dev_ms]
    barrier = pltpu.get_barrier_semaphore()
    for partner in partners:
        pl.semaphore_signal(barrier, inc=1, device_id=partner, device_id_type=MESH)

    locals_ = [
        pltpu.make_async_copy(src, dst, loc_sem.at[i])
        for i, (src, dst) in enumerate(
            [(enc_hbm, enc_v), (q_hbm, q_v), (k_hbm, k_v), (d_hbm, d_v), (v_hbm, v_v), (w_hbm, wbuf.at[f])]
        )
    ]
    for copy in locals_:
        copy.start()
    pl.semaphore_wait(barrier, len(partners))

    sent = []

    def send(src, dst, ssem, rsem, device):
        copy = pltpu.make_async_remote_copy(
            src_ref=src, dst_ref=dst, send_sem=ssem, recv_sem=rsem, device_id=device, device_id_type=MESH
        )
        copy.start()
        sent.append(copy)
        return copy

    arrived = set()

    def arrive(inward, key):
        if (id(inward), key) not in arrived:
            arrived.add((id(inward), key))
            inward[key].wait_recv()

    w_in = {}
    w_in[(3, 0)] = send(w_hbm, wbuf.at[f], ws_sem.at[0], wr_sem.at[12], dev_xu)
    w_in[(1, 0)] = send(w_hbm, wbuf.at[f], ws_sem.at[1], wr_sem.at[4], dev_xd)
    for dz in (1, 3, 2):
        back = (Z - dz) % Z
        w_in[(0, back)] = send(w_hbm, wbuf.at[f], ws_sem.at[1 + dz], wr_sem.at[back], dev_z[dz])

    def w_column(dz):
        arrive(w_in, (0, dz))
        slot = x * Z + (z + dz) % Z
        w_in[(3, dz)] = send(wbuf.at[slot], wbuf.at[slot], ws_sem.at[4 + dz], wr_sem.at[12 + dz], dev_xu)
        w_in[(1, dz)] = send(wbuf.at[slot], wbuf.at[slot], ws_sem.at[7 + dz], wr_sem.at[4 + dz], dev_xd)

    def w_far(dz):
        if dz < 2:
            arrive(w_in, (3, dz))
            slot = x_down * Z + (z + dz) % Z
            to = dev_xu
        else:
            arrive(w_in, (1, dz))
            slot = x_up * Z + (z + dz) % Z
            to = dev_xd
        w_in[(2, dz)] = send(wbuf.at[slot], wbuf.at[slot], ws_sem.at[11 + dz], wr_sem.at[8 + dz], to)

    locals_[0].wait()
    enc_t = enc_v[...].astype(F32).T.astype(BF)
    et[0] = enc_t[:64]
    et[1] = enc_t[64:]
    ebuf[g, :, 0:256] = et[c]
    e_pair = send(et.at[sister], ebuf.at[g, :, pl.ds(256, 256)], es_sem.at[0], er_sem.at[16], dev_s)
    e_in = {}

    def e_out(up, dy, dm):
        slot = ((y + dy) % Y) * 2 + (m_other if dm else m)
        if up:
            there = (dy + Y - 1) % Y
            number = 2 + ((Y - dy) % Y) * 2 + dm
        else:
            there = dy + 1
            number = 10 + dy * 2 + dm
        e_in[(there, dm)] = send(
            ebuf.at[slot], ebuf.at[slot], es_sem.at[number], er_sem.at[there * 2 + dm], dev_yu if up else dev_yd
        )

    def e_own():
        e_pair.wait_recv()
        e_in[(0, 1)] = send(ebuf.at[g], ebuf.at[g], es_sem.at[1], er_sem.at[1], dev_m)
        e_out(True, 0, 0)
        e_out(False, 0, 0)

    def e_other():
        arrive(e_in, (0, 1))
        e_out(True, 0, 1)
        e_out(False, 0, 1)

    def e_step(k, dm):
        if k < 3 or dm == 0:
            arrive(e_in, (Y - k, dm))
            e_out(True, Y - k, dm)
        if k < 3 or dm == 1:
            arrive(e_in, (k, dm))
            e_out(False, k, dm)

    scale = HD ** (-0.5)
    length = len_ref[0]
    valid = lax.broadcasted_iota(jnp.int32, (128, 256), 1) < length

    def head(h):
        cols = slice(h * HD, (h + 1) * HD)
        qh, kh, vh, dh = q_v[:, cols], k_v[:, cols], v_v[:, cols], d_v[:, cols]
        scores = dot(qh, kh, NT) * scale
        scores = jnp.where(valid, scores, NEG_FILL)
        top = jnp.max(scores, axis=-1, keepdims=True)
        expo = jnp.exp(scores - top)
        probs = expo / jnp.sum(expo, axis=-1, keepdims=True)
        dprobs = dot(dh, vh, NT)
        delta = jnp.sum(probs * dprobs, axis=-1, keepdims=True)
        dscore = probs * (dprobs - delta) * scale
        qg_ref[:, cols] = dot(dscore.astype(BF), kh, NN).astype(BF)
        kg[0, :, cols] = dot(dscore.T.astype(BF), qh, NN).astype(BF)

    locals_[1].wait()
    locals_[2].wait()
    locals_[3].wait()
    locals_[4].wait()
    head(0)
    e_own()
    head(1)
    w_column(1)
    head(2)
    w_column(3)
    head(3)
    k_pair = send(kg.at[0], kg.at[1], ks_sem.at[0], kr_sem.at[0], dev_s)
    e_other()
    e_step(1, 0)
    w_far(0)
    w_column(2)
    e_step(1, 1)
    e_step(2, 0)
    w_far(1)
    w_far(3)
    e_step(2, 1)
    e_step(3, 0)
    w_far(2)
    e_step(3, 1)

    k_pair.wait_recv()
    for key in sorted(e_in):
        arrive(e_in, key)

    grads = kg[...].reshape(512, 1024)

    def wg_dot(xt):
        rows = ebuf[pl.ds(xt * Z, Z)].reshape(256, 512)
        part[pl.ds(xt * Z, Z)] = dot(rows, grads, NN).reshape(Z, 64, 1024)

    x_far = (x + 2) % X
    wg_dot(x_far)
    a_in, b_in = {}, {}
    for up in (1, 0):
        for j in range(2):
            zt = j if up else 2 + j
            a_send[up, j] = part[x_far * Z + zt].astype(BF)
            a_in[(up, j)] = send(
                a_send.at[up, j], a_recv.at[up, j], as_sem.at[up * 2 + j], ar_sem.at[up * 2 + j],
                dev_xu if up else dev_xd,
            )

    def b_out(up, zt, value):
        b_send[up, zt] = value.astype(BF)
        b_in[(up, zt)] = send(
            b_send.at[up, zt], b_recv.at[up, zt], bs_sem.at[up * 4 + zt], br_sem.at[up * 4 + zt],
            dev_xu if up else dev_xd,
        )

    wg_dot(x_up)
    for zt in (2, 3):
        b_out(1, zt, part[x_up * Z + zt])
    wg_dot(x_down)
    for zt in (0, 1):
        b_out(0, zt, part[x_down * Z + zt])
    wg_dot(x)

    locals_[5].wait()
    for key in sorted(w_in):
        arrive(w_in, key)

    def eg_dot(yt):
        rows = wbuf[pl.ds(yt * 2, 2)].reshape(128, 1024)
        term[pl.ds(yt * 2, 2)] = dot(rows, grads, NT).reshape(2, 64, 512)

    t_in = {}

    def t_out(up, k, half):
        yt = (y + k) % Y if up else (y + Y - k) % Y
        value = term[yt * 2 + half]
        first = 4 if half != up else 3
        if k < first:
            arrive(t_in, (up, k + 1, half))
            value = value + e_recv[up, k, half].astype(F32)
        e_send[up, k - 1, half] = value.astype(BF)
        number = (up * 4 + k - 1) * 2 + half
        t_in[(up, k, half)] = send(
            e_send.at[up, k - 1, half], e_recv.at[up, k - 1, half], ts_sem.at[number], tr_sem.at[number],
            dev_yu if up else dev_yd,
        )

    eg_dot((y + 4) % Y)
    t_out(1, 4, 0)
    t_out(0, 4, 1)
    eg_dot((y + 3) % Y)
    t_out(1, 3, 1)
    eg_dot((y + 5) % Y)
    t_out(0, 3, 0)
    eg_dot((y + 2) % Y)
    eg_dot((y + 6) % Y)

    def b_sum(up, j):
        zt = j if up else 2 + j
        arrive(a_in, (up, j))
        b_out(up, zt, part[(x_up if up else x_down) * Z + zt] + a_recv[up, j].astype(F32))

    b_sum(1, 0)
    b_sum(0, 0)
    t_out(1, 3, 0)
    t_out(0, 3, 1)
    eg_dot((y + 1) % Y)
    eg_dot((y + 7) % Y)
    b_sum(1, 1)
    b_sum(0, 1)
    t_out(1, 2, 1)
    t_out(0, 2, 0)
    eg_dot(y)
    t_out(1, 2, 0)
    t_out(0, 2, 1)
    t_out(1, 1, 1)
    t_out(0, 1, 0)
    t_out(1, 1, 0)
    t_out(0, 1, 1)

    for up in (1, 0):
        for zt in range(Z):
            arrive(b_in, (up, zt))

    def x_sum(zt):
        return part[x * Z + zt] + b_recv[1, zt].astype(F32) + b_recv[0, zt].astype(F32)

    z_in = {}
    for dz in (2, 1, 3):
        zt = (z + dz) % Z
        z_send[dz - 1] = x_sum(zt).astype(BF)
        back = Z - dz
        z_in[back] = send(z_send.at[dz - 1], z_recv.at[back - 1], zs_sem.at[dz - 1], zr_sem.at[back - 1], dev_z[dz])
    own = x_sum(z)

    for up in (1, 0):
        for half in range(2):
            arrive(t_in, (up, 1, half))

    def y_sum(half):
        return term[y * 2 + half] + e_recv[1, 0, half].astype(F32) + e_recv[0, 0, half].astype(F32)

    away = y_sum(m_other).astype(BF)
    e_last[0] = away[:, 0:256]
    e_last[1] = away[:, 256:512]
    l_in = [
        send(e_last.at[0], fin.at[0], ls_sem.at[0], lr_sem.at[0], dev_m),
        send(e_last.at[1], fin.at[1], ls_sem.at[1], lr_sem.at[1], dev_ms),
    ]
    home = y_sum(m)
    e_last[2] = home[:, 256:512].astype(BF)
    l_in.append(send(e_last.at[2], fin.at[2], ls_sem.at[2], lr_sem.at[2], dev_s))

    for back in (2, 1, 3):
        arrive(z_in, back)
    own = own + z_recv[0].astype(F32) + z_recv[1].astype(F32) + z_recv[2].astype(F32)
    wg_ref[...] = own * (1.0 / 32)

    for copy in l_in:
        copy.wait_recv()
    enc_sum[c] = home[:, 0:256] + fin[0].astype(F32)
    enc_sum[sister] = fin[1].astype(F32) + fin[2].astype(F32)
    eg_ref[...] = enc_sum[...].reshape(128, 256).T.astype(BF)

    for copy in sent:
        copy.wait_send()


def shards(queries, keys, values, out_grad, key_weight, encoded, enc_lengths):
    dma = pltpu.SemaphoreType.DMA
    anywhere = pl.BlockSpec(memory_space=pl.ANY)
    vmem = pl.BlockSpec(memory_space=pltpu.VMEM)
    query_grad, encoder_grad, weight_grad = pl.pallas_call(
        kernel,
        out_shape=(
            jax.ShapeDtypeStruct((128, 1024), BF),
            jax.ShapeDtypeStruct((256, 128), BF),
            jax.ShapeDtypeStruct((64, 1024), F32),
        ),
        in_specs=[anywhere] * 6 + [pl.BlockSpec(memory_space=pltpu.SMEM)],
        out_specs=(vmem, vmem, vmem),
        scratch_shapes=[
            pltpu.VMEM((128, 1024), BF),
            pltpu.VMEM((256, 1024), BF),
            pltpu.VMEM((256, 1024), BF),
            pltpu.VMEM((128, 1024), BF),
            pltpu.VMEM((256, 128), BF),
            pltpu.VMEM((2, 64, 256), BF),
            pltpu.VMEM((F, 64, 512), BF),
            pltpu.VMEM((F, 64, 1024), BF),
            pltpu.VMEM((2, 256, 1024), BF),
            pltpu.VMEM((F, 64, 512), F32),
            pltpu.VMEM((2, 4, 2, 64, 512), BF),
            pltpu.VMEM((2, 4, 2, 64, 512), BF),
            pltpu.VMEM((3, 64, 256), BF),
            pltpu.VMEM((3, 64, 256), BF),
            pltpu.VMEM((2, 64, 256), F32),
            pltpu.VMEM((F, 64, 1024), F32),
            pltpu.VMEM((2, 2, 64, 1024), BF),
            pltpu.VMEM((2, 2, 64, 1024), BF),
            pltpu.VMEM((2, 4, 64, 1024), BF),
            pltpu.VMEM((2, 4, 64, 1024), BF),
            pltpu.VMEM((3, 64, 1024), BF),
            pltpu.VMEM((3, 64, 1024), BF),
            dma((6,)), dma((15,)), dma((16,)), dma((18,)), dma((17,)), dma((1,)), dma((1,)),
            dma((16,)), dma((16,)), dma((3,)), dma((3,)), dma((4,)), dma((4,)), dma((8,)), dma((8,)),
            dma((3,)), dma((3,)),
        ],
        compiler_params=pltpu.CompilerParams(
            collective_id=0, has_side_effects=True, vmem_limit_bytes=48 * 1024 * 1024
        ),
    )(queries[0], keys[0], values[0], out_grad[0], key_weight[0], encoded, enc_lengths)
    return (query_grad[None], encoder_grad, weight_grad[None])


def solution(mesh):
    placed = (
        P("section", "dp", "mp"),
        P("section", "dp", "mp"),
        P("section", "dp", "mp"),
        P("section", "dp", "mp"),
        P("section", "dp", "mp"),
        P("dp", ("section", "mp")),
        P("dp"),
    )
    return jax.shard_map(
        shards,
        mesh=mesh,
        in_specs=placed,
        out_specs=(P("section", "dp", "mp"), P("dp", ("section", "mp")), P("section", "dp", "mp")),
        check_vma=False,
    )
```

```python
import jax
import jax.numpy as jnp
from jax import lax
from jax.experimental import pallas as pl
from jax.experimental.pallas import tpu as pltpu
from jax.sharding import PartitionSpec as P

HD = 256
NEG_FILL = -1e30
X, Z, Y = 4, 4, 8
F = X * Z
MESH = pl.DeviceIdType.MESH
BF = jnp.bfloat16
F32 = jnp.float32

NT = (((1,), (1,)), ((), ()))
NN = (((1,), (0,)), ((), ()))
TN = (((0,), (0,)), ((), ()))


def dot(a, b, dims):
    return lax.dot_general(a, b, dims, preferred_element_type=F32)


def kernel(
    q_hbm, k_hbm, v_hbm, d_hbm, w_hbm, enc_hbm, len_hbm,
    qg_ref, eg_ref, wg_ref,
    q_v, k_v, v_v, d_v, enc_v, len_ref, et, ebuf, wbuf, kg,
    term, e_send, e_recv, e_last, fin, enc_sum,
    part, a_send, a_recv, b_send, b_recv, z_send, z_recv,
    loc_sem, ws_sem, wr_sem, es_sem, er_sem, ks_sem, kr_sem,
    ts_sem, tr_sem, ls_sem, lr_sem, as_sem, ar_sem, bs_sem, br_sem, zs_sem, zr_sem,
):
    dp = lax.axis_index("dp")
    y = lax.axis_index("section")
    m = lax.axis_index("mp")
    x = dp // 8
    z = (dp // 2) % 4
    c = dp % 2
    f = dp // 2
    g = y * 2 + m

    def dev(x=x, z=z, c=c, y=y, m=m):
        return {"dp": x * 8 + z * 2 + c, "section": y, "mp": m}

    x_up, x_down = (x + 1) % X, (x + X - 1) % X
    y_up, y_down = (y + 1) % Y, (y + Y - 1) % Y
    sister, m_other = 1 - c, 1 - m
    dev_xu, dev_xd, dev_x2 = dev(x=x_up), dev(x=x_down), dev(x=(x + 2) % X)
    dev_yu, dev_yd = dev(y=y_up), dev(y=y_down)
    dev_yu2, dev_yd2 = dev(y=(y + 2) % Y), dev(y=(y + Y - 2) % Y)
    z_other = [z, z + 1 - 2 * (z % 2), (z + 2) % Z, Z - 1 - z]
    dev_z = [dev(z=other) for other in z_other]
    dev_s, dev_m, dev_ms = dev(c=sister), dev(m=m_other), dev(c=sister, m=m_other)

    loads = [
        pltpu.make_async_copy(src, dst, loc_sem.at[i])
        for i, (src, dst) in enumerate(
            [(enc_hbm, enc_v), (q_hbm, q_v), (k_hbm, k_v), (d_hbm, d_v), (v_hbm, v_v), (w_hbm, wbuf.at[f]),
             (len_hbm, len_ref)]
        )
    ]

    partners = [dev_xu, dev_xd, dev_x2, dev_yu, dev_yd, dev_yu2, dev_yd2] + dev_z[1:] + [dev_s, dev_m, dev_ms]
    barrier = pltpu.get_barrier_semaphore()
    for partner in partners:
        pl.semaphore_signal(barrier, inc=1, device_id=partner, device_id_type=MESH)
    for copy in loads:
        copy.start()
    loads[0].wait()
    enc_t = enc_v[...].astype(F32).T.astype(BF)
    et[0] = enc_t[:64]
    et[1] = enc_t[64:]
    ebuf[g, :, 0:256] = et[c]
    pl.semaphore_wait(barrier, len(partners))

    sent = []

    def send(src, dst, ssem, rsem, device):
        copy = pltpu.make_async_remote_copy(
            src_ref=src, dst_ref=dst, send_sem=ssem, recv_sem=rsem, device_id=device, device_id_type=MESH
        )
        copy.start()
        sent.append(copy)
        return copy

    arrived = set()

    def arrive(inward, key):
        if (id(inward), key) not in arrived:
            arrived.add((id(inward), key))
            inward[key].wait_recv()

    e_in, w_in = {}, {}
    e_in["mine"] = send(et.at[sister], ebuf.at[g, :, pl.ds(256, 256)], es_sem.at[0], er_sem.at[0], dev_s)
    e_in["same"] = send(et.at[c], ebuf.at[g, :, pl.ds(0, 256)], es_sem.at[1], er_sem.at[1], dev_m)
    e_in["cross"] = send(et.at[sister], ebuf.at[g, :, pl.ds(256, 256)], es_sem.at[16], er_sem.at[16], dev_ms)

    w_in[(3, 0)] = send(w_hbm, wbuf.at[f], ws_sem.at[0], wr_sem.at[12], dev_xu)
    w_in[(1, 0)] = send(w_hbm, wbuf.at[f], ws_sem.at[1], wr_sem.at[4], dev_xd)
    for k in (1, 3):
        w_in[(0, k)] = send(w_hbm, wbuf.at[f], ws_sem.at[1 + k], wr_sem.at[k], dev_z[k])
    w_in[(2, 0)] = send(w_hbm, wbuf.at[f], ws_sem.at[3], wr_sem.at[8], dev_x2)

    inner = z * (3 - z) > 0

    def w_relay(k):
        arrive(w_in, (0, k))
        slot = x * Z + z_other[k]
        copy = pltpu.make_async_remote_copy(
            src_ref=wbuf.at[slot], dst_ref=wbuf.at[slot], send_sem=ws_sem.at[18 + k // 2], recv_sem=wr_sem.at[2],
            device_id=dev_z[4 - k], device_id_type=MESH,
        )
        w_in[(0, 2)] = copy
        relayed.append(copy)

        @pl.when(inner)
        def _():
            copy.start()

    relayed = []

    def w_column(k):
        arrive(w_in, (0, k))
        slot = x * Z + z_other[k]
        w_in[(3, k)] = send(wbuf.at[slot], wbuf.at[slot], ws_sem.at[4 + k], wr_sem.at[12 + k], dev_xu)
        w_in[(1, k)] = send(wbuf.at[slot], wbuf.at[slot], ws_sem.at[7 + k], wr_sem.at[4 + k], dev_xd)

    def w_far(k):
        arrive(w_in, (3, k))
        half = wbuf.at[x_down * Z + z_other[k], pl.ds(0, 32)]
        w_in[(2, k)] = send(half, half, ws_sem.at[10 + k], wr_sem.at[8 + k], dev_xu)
        arrive(w_in, (1, k))
        half = wbuf.at[x_up * Z + z_other[k], pl.ds(32, 32)]
        w_in[(6, k)] = send(half, half, ws_sem.at[13 + k], wr_sem.at[16 + k], dev_xd)

    def e_out(number, dy, dm, step):
        slot = ((y + dy) % Y) * 2 + (m_other if dm else m)
        there = (dy - step) % Y
        to = {1: dev_yu, 2: dev_yu2, -1: dev_yd, -2: dev_yd2}[step]
        e_in[(there, dm)] = send(ebuf.at[slot], ebuf.at[slot], es_sem.at[number], er_sem.at[there * 2 + dm], to)

    def e_own():
        arrive(e_in, "mine")
        e_out(2, 0, 0, 1)
        e_out(3, 0, 0, -1)

    def e_ring(k):
        arrive(e_in, (Y - k, 0))
        e_out(4 + 2 * k, Y - k, 0, 1)
        if k < 3:
            arrive(e_in, (k, 0))
            e_out(5 + 2 * k, k, 0, -1)

    def e_other():
        arrive(e_in, "same")
        arrive(e_in, "cross")
        for i, step in enumerate((2, -2, 1, -1)):
            e_out(17 + i, 0, 1, step)

    def e_far():
        arrive(e_in, (2, 1))
        e_out(21, 2, 1, -2)
        e_out(22, 2, 1, -1)
        arrive(e_in, (6, 1))
        e_out(23, 6, 1, 1)

    scale = HD ** (-0.5)

    def head(h):
        cols = slice(h * HD, (h + 1) * HD)
        qh, kh, vh, dh = q_v[:, cols], k_v[:, cols], v_v[:, cols], d_v[:, cols]
        scores = dot(qh, kh, NT) * scale
        scores = jnp.where(valid, scores, NEG_FILL)
        top = jnp.max(scores, axis=-1, keepdims=True)
        expo = jnp.exp(scores - top)
        probs = expo / jnp.sum(expo, axis=-1, keepdims=True)
        dprobs = dot(dh, vh, NT)
        delta = jnp.sum(probs * dprobs, axis=-1, keepdims=True)
        dscore = probs * (dprobs - delta) * scale
        qg_ref[:, cols] = dot(dscore.astype(BF), kh, NN).astype(BF)
        kg[0, :, cols] = dot(dscore.T.astype(BF), qh, NN).astype(BF)

    for copy in loads[1:]:
        copy.wait()
    valid = lax.broadcasted_iota(jnp.int32, (128, 256), 1) < len_ref[0:1, :]
    head(0)
    e_own()
    head(1)
    head(2)
    w_relay(1)
    w_column(1)
    e_ring(1)
    head(3)
    k_pair = send(kg.at[0], kg.at[1], ks_sem.at[0], kr_sem.at[0], dev_s)
    e_other()
    w_relay(3)
    w_column(3)
    e_ring(2)
    w_column(2)
    w_far(1)
    e_ring(3)
    w_far(3)
    e_far()
    w_far(2)

    k_pair.wait_recv()
    for key in list(e_in):
        arrive(e_in, key)

    grads = kg[...].reshape(512, 1024)

    def wg_dot(xt):
        rows = ebuf[pl.ds(xt * Z, Z)].reshape(256, 512)
        part[pl.ds(xt * Z, Z)] = dot(rows, grads, NN).reshape(Z, 64, 1024)

    a_in, b_in, z_in = {}, {}, {}
    x_far = (x + 2) % X

    def a_out(up, k):
        a_send[k] = part[x_far * Z + z_other[k]].astype(BF)
        a_in[k] = send(a_send.at[k], a_recv.at[k], as_sem.at[k], ar_sem.at[k], dev_xu if up else dev_xd)

    def b_out(up, k):
        value = part[(x_up if up else x_down) * Z + z_other[k]]
        if up == k % 2:
            arrive(a_in, k)
            value = value + a_recv[k].astype(F32)
        b_send[up, k] = value.astype(BF)
        b_in[(up, k)] = send(
            b_send.at[up, k], b_recv.at[up, k], bs_sem.at[up * 4 + k], br_sem.at[up * 4 + k],
            dev_xu if up else dev_xd,
        )

    def x_sum(k):
        arrive(b_in, (1, k))
        arrive(b_in, (0, k))
        return part[x * Z + z_other[k]] + b_recv[1, k].astype(F32) + b_recv[0, k].astype(F32)

    def z_out(k):
        z_send[k - 1] = x_sum(k).astype(BF)
        z_in[k] = send(z_send.at[k - 1], z_recv.at[k - 1], zs_sem.at[k - 1], zr_sem.at[k - 1], dev_z[k])

    wg_dot(x_far)
    a_out(1, 3)
    a_out(0, 2)
    wg_dot(x_up)
    b_out(1, 2)
    wg_dot(x_down)
    b_out(0, 3)

    for key in list(w_in):
        arrive(w_in, key)

    def eg_dot(yt):
        rows = wbuf[pl.ds(yt * 2, 2)].reshape(128, 1024)
        term[pl.ds(yt * 2, 2)] = dot(rows, grads, NT).reshape(2, 64, 512)

    t_in = {}

    def t_out(up, k, half):
        yt = (y + k) % Y if up else (y + Y - k) % Y
        value = term[yt * 2 + half]
        first = 4 if half != up else 3
        if k < first:
            arrive(t_in, (up, k + 1, half))
            value = value + e_recv[up, k, half].astype(F32)
        e_send[up, k - 1, half] = value.astype(BF)
        number = (up * 4 + k - 1) * 2 + half
        t_in[(up, k, half)] = send(
            e_send.at[up, k - 1, half], e_recv.at[up, k - 1, half], ts_sem.at[number], tr_sem.at[number],
            dev_yu if up else dev_yd,
        )

    eg_dot((y + 4) % Y)
    t_out(1, 4, 0)
    t_out(0, 4, 1)
    eg_dot((y + 3) % Y)
    t_out(1, 3, 1)
    eg_dot((y + 5) % Y)
    t_out(0, 3, 0)
    b_out(1, 3)
    b_out(0, 2)
    a_out(1, 1)
    a_out(0, 0)
    eg_dot((y + 2) % Y)
    eg_dot((y + 6) % Y)
    t_out(1, 3, 0)
    t_out(0, 3, 1)
    t_out(1, 2, 1)
    t_out(0, 2, 0)
    b_out(1, 0)
    b_out(0, 1)
    eg_dot((y + 1) % Y)
    eg_dot((y + 7) % Y)
    wg_dot(x)
    t_out(1, 2, 0)
    t_out(0, 2, 1)
    z_out(3)
    z_out(2)
    t_out(1, 1, 1)
    t_out(0, 1, 0)
    b_out(1, 1)
    b_out(0, 0)
    eg_dot(y)
    t_out(1, 1, 0)
    t_out(0, 1, 1)

    for up in (1, 0):
        for half in range(2):
            arrive(t_in, (up, 1, half))

    def y_sum(half):
        return term[y * 2 + half] + e_recv[1, 0, half].astype(F32) + e_recv[0, 0, half].astype(F32)

    away = y_sum(m_other).astype(BF)
    e_last[0] = away[:, 0:256]
    e_last[1] = away[:, 256:512]
    l_in = [
        send(e_last.at[0], fin.at[0], ls_sem.at[0], lr_sem.at[0], dev_m),
        send(e_last.at[1], fin.at[1], ls_sem.at[1], lr_sem.at[1], dev_ms),
    ]
    home = y_sum(m)
    e_last[2] = home[:, 256:512].astype(BF)
    l_in.append(send(e_last.at[2], fin.at[2], ls_sem.at[2], lr_sem.at[2], dev_s))

    z_out(1)
    own = x_sum(0)
    for copy in l_in:
        copy.wait_recv()
    enc_sum[c] = home[:, 0:256] + fin[0].astype(F32)
    enc_sum[sister] = fin[1].astype(F32) + fin[2].astype(F32)
    eg_ref[...] = enc_sum[...].reshape(128, 256).T.astype(BF)

    for k in (3, 2, 1):
        arrive(z_in, k)
        own = own + z_recv[k - 1].astype(F32)
    wg_ref[...] = own * (1.0 / 32)

    for copy in sent:
        copy.wait_send()

    @pl.when(inner)
    def _():
        for copy in relayed:
            copy.wait_send()


def shards(queries, keys, values, out_grad, key_weight, encoded, enc_lengths):
    dma = pltpu.SemaphoreType.DMA
    anywhere = pl.BlockSpec(memory_space=pltpu.HBM)
    vmem = pl.BlockSpec(memory_space=pltpu.VMEM)
    held = [
        pltpu.with_memory_space_constraint(array, pltpu.HBM)
        for array in (queries[0], keys[0], values[0], out_grad[0], key_weight[0], encoded)
    ]
    query_grad, encoder_grad, weight_grad = pl.pallas_call(
        kernel,
        out_shape=(
            jax.ShapeDtypeStruct((128, 1024), BF),
            jax.ShapeDtypeStruct((256, 128), BF),
            jax.ShapeDtypeStruct((64, 1024), F32),
        ),
        in_specs=[anywhere] * 7,
        out_specs=(vmem, vmem, vmem),
        scratch_shapes=[
            pltpu.VMEM((128, 1024), BF),
            pltpu.VMEM((256, 1024), BF),
            pltpu.VMEM((256, 1024), BF),
            pltpu.VMEM((128, 1024), BF),
            pltpu.VMEM((256, 128), BF),
            pltpu.VMEM((8, 256), jnp.int32),
            pltpu.VMEM((2, 64, 256), BF),
            pltpu.VMEM((F, 64, 512), BF),
            pltpu.VMEM((F, 64, 1024), BF),
            pltpu.VMEM((2, 256, 1024), BF),
            pltpu.VMEM((F, 64, 512), F32),
            pltpu.VMEM((2, 4, 2, 64, 512), BF),
            pltpu.VMEM((2, 4, 2, 64, 512), BF),
            pltpu.VMEM((3, 64, 256), BF),
            pltpu.VMEM((3, 64, 256), BF),
            pltpu.VMEM((2, 64, 256), F32),
            pltpu.VMEM((F, 64, 1024), F32),
            pltpu.VMEM((4, 64, 1024), BF),
            pltpu.VMEM((4, 64, 1024), BF),
            pltpu.VMEM((2, 4, 64, 1024), BF),
            pltpu.VMEM((2, 4, 64, 1024), BF),
            pltpu.VMEM((3, 64, 1024), BF),
            pltpu.VMEM((3, 64, 1024), BF),
            dma((7,)), dma((21,)), dma((20,)), dma((24,)), dma((17,)), dma((1,)), dma((1,)),
            dma((16,)), dma((16,)), dma((3,)), dma((3,)), dma((4,)), dma((4,)), dma((8,)), dma((8,)),
            dma((3,)), dma((3,)),
        ],
        compiler_params=pltpu.CompilerParams(
            collective_id=0, has_side_effects=True, vmem_limit_bytes=48 * 1024 * 1024
        ),
    )(*held, jnp.broadcast_to(enc_lengths[:, None], (8, 256)))
    return (query_grad[None], encoder_grad, weight_grad[None])


def solution(mesh):
    placed = (
        P("section", "dp", "mp"),
        P("section", "dp", "mp"),
        P("section", "dp", "mp"),
        P("section", "dp", "mp"),
        P("section", "dp", "mp"),
        P("dp", ("section", "mp")),
        P("dp"),
    )
    return jax.shard_map(
        shards,
        mesh=mesh,
        in_specs=placed,
        out_specs=(P("section", "dp", "mp"), P("dp", ("section", "mp")), P("section", "dp", "mp")),
        check_vma=False,
    )
```

```python
import jax
import jax.numpy as jnp
from jax import lax
from jax.experimental import pallas as pl
from jax.experimental.pallas import tpu as pltpu
from jax.sharding import PartitionSpec as P

HD = 256
NEG_FILL = -1e30
X, Z, Y = 4, 4, 8
F = X * Z
MESH = pl.DeviceIdType.MESH
BF = jnp.bfloat16
F32 = jnp.float32

NT = (((1,), (1,)), ((), ()))
NN = (((1,), (0,)), ((), ()))
TN = (((0,), (0,)), ((), ()))


def dot(a, b, dims):
    return lax.dot_general(a, b, dims, preferred_element_type=F32)


def kernel(
    q_hbm, k_hbm, v_hbm, d_hbm, w_hbm, enc_hbm, len_hbm,
    qg_ref, eg_ref, wg_ref,
    q_v, k_v, v_v, d_v, enc_v, len_v, et, ebuf, wbuf, kg,
    term, t_send, t_recv, l_send, l_recv, enc_sum,
    part, a_send, a_recv, b_send, b_recv, z_send, z_recv,
    loc_sem, ws_sem, wr_sem, es_sem, er_sem, ks_sem, kr_sem,
    ts_sem, tr_sem, ls_sem, lr_sem, as_sem, ar_sem, bs_sem, br_sem, zs_sem, zr_sem,
):
    dp = lax.axis_index("dp")
    y = lax.axis_index("section")
    m = lax.axis_index("mp")
    x = dp // 8
    z = (dp // 2) % 4
    c = dp % 2
    q = z % 2
    f = dp // 2

    def dev(x=x, z=z, c=c, y=y, m=m):
        return {"dp": x * 8 + z * 2 + c, "section": y, "mp": m}

    z_other = [z, z + 1 - 2 * q, (z + 2) % Z, Z - 1 - z]
    sister, m_other = 1 - c, 1 - m
    dev_x = [dev(x=(x + dx) % X) for dx in range(X)]
    dev_y = {step: dev(y=(y + Y + step) % Y) for step in (1, -1, 2, -2)}
    dev_z = [dev(z=other) for other in z_other]
    group = [dict(), dict(c=sister), dict(z=z_other[1]), dict(c=sister, z=z_other[1])]
    quarter = [c * 2 + q, sister * 2 + q, c * 2 + 1 - q, sister * 2 + 1 - q]
    dev_home = [dev(**other) for other in group]
    dev_away = [dev(m=m_other, **other) for other in group]

    loads = [
        pltpu.make_async_copy(src, dst, loc_sem.at[i])
        for i, (src, dst) in enumerate(
            [(enc_hbm, enc_v), (q_hbm, q_v), (k_hbm, k_v), (d_hbm, d_v), (v_hbm, v_v),
             (w_hbm.at[pl.ds(pl.multiple_of(q * 32, 32), 32)], wbuf.at[f]), (len_hbm, len_v)]
        )
    ]

    partners = dev_x[1:] + list(dev_y.values()) + dev_z[2:] + dev_home[1:] + dev_away
    barrier = pltpu.get_barrier_semaphore()
    for partner in partners:
        pl.semaphore_signal(barrier, inc=1, device_id=partner, device_id_type=MESH)
    for copy in loads:
        copy.start()
    loads[0].wait()
    et[...] = enc_v[...].astype(F32).T.astype(BF).reshape(4, 32, 256)
    ebuf[y, m, :, 0:256] = et[quarter[0]]
    pl.semaphore_wait(barrier, len(partners))

    sent = []

    def send(src, dst, ssem, rsem, device):
        copy = pltpu.make_async_remote_copy(
            src_ref=src, dst_ref=dst, send_sem=ssem, recv_sem=rsem, device_id=device, device_id_type=MESH
        )
        copy.start()
        sent.append(copy)
        return copy

    arrived = set()

    def arrive(inward, key):
        if (id(inward), key) not in arrived:
            arrived.add((id(inward), key))
            inward[key].wait_recv()

    e_in, w_in, k_in = {}, {}, {}

    def e_piece(across, j):
        number = 18 + across * 4 + j
        e_in[("piece", across, j)] = send(
            et.at[quarter[j]], ebuf.at[y, m, :, pl.ds(j * 256, 256)], es_sem.at[number], er_sem.at[number],
            dev_away[j] if across else dev_home[j],
        )

    def w_send(src, dst, dx, k, to):
        number = dx * 4 + k
        w_in[(dx, k)] = send(src, dst, ws_sem.at[number], wr_sem.at[number], to)

    def w_rows(half):
        return w_hbm.at[pl.ds(pl.multiple_of(half * 32, 32), 32)]

    def w_own():
        w_own_z()
        w_own_x()

    def w_own_z():
        for k in (1, 3, 2):
            w_send(w_rows(q if k == 2 else 1 - q), wbuf.at[f], 0, k, dev_z[k])

    def w_own_x():
        for dx in (1, 3, 2):
            w_send(w_rows(q), wbuf.at[f], X - dx, 0, dev_x[dx])

    def w_column(k):
        arrive(w_in, (0, k))
        slot = wbuf.at[x * Z + z_other[k]]
        for dx in (1, 3, 2):
            w_send(slot, slot, X - dx, k, dev_x[dx])

    def e_out(dm, dy, step, rows=None, number=None):
        slot = ebuf.at[(y + dy) % Y, m_other if dm else m]
        if rows is not None:
            slot = slot.at[pl.ds(rows, 16)]
        there = (dy - step) % Y
        if number is None:
            number = there
        e_in[(dm, number)] = send(
            slot, slot, es_sem.at[dm * 9 + number], er_sem.at[dm * 9 + number], dev_y[step]
        )

    def e_first(dm):
        for j in range(1 - dm, 4):
            arrive(e_in, ("piece", dm, j))
        e_out(dm, 0, 2)
        e_out(dm, 0, -2)

    def e_near(dm):
        e_out(dm, 0, 1)
        e_out(dm, 0, -1)

    def e_far(dm):
        arrive(e_in, (dm, 6))
        e_out(dm, 6, 2, 0, 4)
        e_out(dm, 6, 1)
        arrive(e_in, (dm, 2))
        e_out(dm, 2, -2, 16, 8)
        e_out(dm, 2, -1)

    def e_all(dm):
        for number in (1, 7, 2, 6, 3, 5, 4, 8):
            arrive(e_in, (dm, number))

    scale = HD ** (-0.5)

    def head(h):
        cols = slice(h * HD, (h + 1) * HD)
        qh, kh, vh, dh = q_v[:, cols], k_v[:, cols], v_v[:, cols], d_v[:, cols]
        scores = dot(qh, kh, NT) * scale
        scores = jnp.where(valid, scores, NEG_FILL)
        top = jnp.max(scores, axis=-1, keepdims=True)
        expo = jnp.exp(scores - top)
        probs = expo / jnp.sum(expo, axis=-1, keepdims=True)
        dprobs = dot(dh, vh, NT)
        delta = jnp.sum(probs * dprobs, axis=-1, keepdims=True)
        dscore = probs * (dprobs - delta) * scale
        kg[0, :, cols] = dot(dscore.T.astype(BF), qh, NN).astype(BF)
        k_send(2, h, 0, 2)
        k_send(1, h, 0, 1)
        qg_ref[:, cols] = dot(dscore.astype(BF), kh, NN).astype(BF)

    def k_send(j, h, src, to):
        cols = pl.ds(h * HD, HD)
        number = (j - 1) * 4 + h
        k_in[(j, h)] = send(
            kg.at[src, :, cols], kg.at[j, :, cols], ks_sem.at[number], kr_sem.at[number], dev_home[to]
        )

    def k_relay(h):
        arrive(k_in, (2, h))
        k_send(3, h, 2, 1)

    def eg_dot(t):
        grads = kg[2 * t : 2 * t + 2].reshape(512, 1024)
        term[t] = dot(wbuf[...].reshape(512, 1024), grads, NT).reshape(F, 32, 512)

    t_in = {}

    def t_out(t, up, k, half):
        yt = (y + k) % Y if up else (y + Y - k) % Y
        value = term[t, yt * 2 + half]
        if k < 3:
            arrive(t_in, (t, up, k + 1, half))
            value = value + t_recv[t, up, k, half].astype(F32)
        if k == 2 and half != up:
            arrive(t_in, (t, up, 4, half))
            value = value + t_recv[t, up, 3, half].astype(F32)
        t_send[t, up, k - 1, half] = value.astype(BF)
        number = ((t * 2 + up) * 4 + k - 1) * 2 + half
        step = 2 if k == 4 else 1
        t_in[(t, up, k, half)] = send(
            t_send.at[t, up, k - 1, half], t_recv.at[t, up, k - 1, half], ts_sem.at[number], tr_sem.at[number],
            dev_y[step if up else -step],
        )

    def eg_start(t):
        t_out(t, 1, 4, 0)
        t_out(t, 0, 4, 1)
        eg_step(t, 3)

    def eg_step(t, k):
        t_out(t, 1, k, 0)
        t_out(t, 0, k, 1)
        t_out(t, 1, k, 1)
        t_out(t, 0, k, 0)

    l_in = {}
    home = {}

    def l_out(across, j, value):
        number = across * 4 + j
        l_send[number] = value.astype(BF)
        l_in[(across, j)] = send(
            l_send.at[number], l_recv.at[number], ls_sem.at[number], lr_sem.at[number],
            dev_away[j] if across else dev_home[j],
        )

    def y_sum(t, half):
        return term[t, y * 2 + half] + t_recv[t, 1, 0, half].astype(F32) + t_recv[t, 0, 0, half].astype(F32)

    def eg_end(t):
        for up in (1, 0):
            for half in range(2):
                arrive(t_in, (t, up, 1, half))
        away = y_sum(t, m_other)
        l_out(1, 2 * t, away[:, 0:256])
        l_out(1, 2 * t + 1, away[:, 256:512])
        total = y_sum(t, m)
        if t == 0:
            home[0] = total[:, 0:256]
        else:
            l_out(0, 2, total[:, 0:256])
        l_out(0, 2 * t + 1, total[:, 256:512])

    first = (q + m) % 2

    def bit(turn):
        return 1 - first if turn else first

    def place(dx, turn, b):
        other = (z + 2 * b) % Z + bit(turn) * (1 - 2 * q)
        return ((x + dx) % X) * 2 + other // 2, other % 2

    def wg_dot(mt):
        rows = ebuf[:, mt].reshape(256, 1024)
        part[:, mt] = dot(rows, kg[...].reshape(1024, 1024), NN).reshape(Y, 32, 1024)

    a_in, b_in = {}, {}

    def a_out(turn, b):
        number = turn * 2 + b
        a_send[number] = part[place(2, turn, b)].astype(BF)
        a_in[number] = send(
            a_send.at[number], a_recv.at[number], as_sem.at[number], ar_sem.at[number], dev_x[1 if b else 3]
        )

    def b_out(turn, b, up):
        number = turn * 2 + b
        value = part[place(1 if up else 3, turn, b)]
        if up == b:
            arrive(a_in, number)
            value = value + a_recv[number].astype(F32)
        slot = up * 4 + number
        b_send[slot] = value.astype(BF)
        b_in[(number, up)] = send(
            b_send.at[slot], b_recv.at[slot], bs_sem.at[slot], br_sem.at[slot], dev_x[1 if up else 3]
        )

    def wg_start(turn):
        a_out(turn, 1)
        a_out(turn, 0)
        b_out(turn, 0, 1)
        b_out(turn, 1, 0)

    def wg_next(turn):
        b_out(turn, 1, 1)
        b_out(turn, 0, 0)

    def x_sum(turn, b, zt):
        number = turn * 2 + b
        return (
            part[x * 2 + zt // 2, zt % 2] + b_recv[number].astype(F32) + b_recv[4 + number].astype(F32)
        )

    def z_copy(k):
        return pltpu.make_async_remote_copy(
            src_ref=z_send.at[k - 1], dst_ref=z_recv.at[k - 1], send_sem=zs_sem.at[k - 1], recv_sem=zr_sem.at[k - 1],
            device_id=dev_z[k], device_id_type=MESH,
        )

    def z_out(turn):
        for up in (1, 0):
            arrive(b_in, (turn * 2 + 1, up))
        k = 2 + bit(turn)
        zt = (z + 2) % Z + bit(turn) * (1 - 2 * q)
        z_send[k - 1] = x_sum(turn, 1, zt).astype(BF)
        send(z_send.at[k - 1], z_recv.at[k - 1], zs_sem.at[k - 1], zr_sem.at[k - 1], dev(z=zt))

    def z_last():
        for turn in (0, 1):
            for up in (1, 0):
                arrive(b_in, (turn * 2, up))
        z_send[0] = x_sum(1 - first, 0, z_other[1]).astype(BF)
        send(z_send.at[0], z_recv.at[0], zs_sem.at[0], zr_sem.at[0], dev_z[1])

    for j in (2, 3, 0, 1):
        e_piece(1, j)
    for j in (2, 3, 1):
        e_piece(0, j)
    w_own()
    for copy in loads[1:]:
        copy.wait()
    valid = lax.broadcasted_iota(jnp.int32, (128, 256), 1) < len_v[0:1, :]
    head(0)
    head(1)
    e_first(0)
    e_near(0)
    head(2)
    head(3)
    w_column(1)
    w_column(3)
    e_first(1)
    w_column(2)
    k_relay(0)
    e_far(0)
    e_near(1)
    k_relay(1)
    e_far(1)
    k_relay(2)
    for key in list(w_in):
        arrive(w_in, key)
    for h in range(4):
        arrive(k_in, (1, h))
    eg_dot(0)
    eg_start(0)
    k_relay(3)
    for key in list(k_in):
        arrive(k_in, key)
    eg_dot(1)
    eg_start(1)
    eg_step(0, 2)
    e_all(0)
    wg_dot(m)
    wg_start(0)
    eg_step(1, 2)
    e_all(1)
    wg_dot(m_other)
    wg_start(1)
    eg_step(0, 1)
    wg_next(0)
    eg_step(1, 1)
    eg_end(0)
    wg_next(1)
    eg_end(1)
    z_out(0)
    z_out(1)
    z_last()

    own = x_sum(first, 0, z)
    z_copy(2).wait_recv()
    wg_ref[pl.ds(pl.multiple_of(q * 32, 32), 32), :] = (own + z_recv[1].astype(F32)) * (1.0 / 32)
    z_copy(1).wait_recv()
    z_copy(3).wait_recv()
    wg_ref[pl.ds(pl.multiple_of((1 - q) * 32, 32), 32), :] = (
        z_recv[0].astype(F32) + z_recv[2].astype(F32)
    ) * (1.0 / 32)

    for key in list(l_in):
        arrive(l_in, key)
    for j in range(4):
        here = home[0] if j == 0 else l_recv[j].astype(F32)
        enc_sum[quarter[j]] = here + l_recv[4 + j].astype(F32)
    eg_ref[...] = enc_sum[...].reshape(128, 256).T.astype(BF)

    for copy in sent:
        copy.wait_send()


def write_out(a, b, c, a_out, b_out, c_out, sems):
    copies = [
        pltpu.make_async_copy(src, dst, sems.at[i])
        for i, (src, dst) in enumerate([(a, a_out), (b, b_out), (c, c_out)])
    ]
    for copy in copies:
        copy.start()
    for copy in copies:
        copy.wait()


def shards(queries, keys, values, out_grad, key_weight, encoded, enc_lengths):
    dma = pltpu.SemaphoreType.DMA
    anywhere = pl.BlockSpec(memory_space=pltpu.HBM)
    vmem = pl.BlockSpec(memory_space=pltpu.VMEM)
    held = [
        pltpu.with_memory_space_constraint(array, pltpu.HBM)
        for array in (queries[0], keys[0], values[0], out_grad[0], key_weight[0], encoded)
    ]
    query_grad, encoder_grad, weight_grad = pl.pallas_call(
        kernel,
        out_shape=(
            jax.ShapeDtypeStruct((128, 1024), BF),
            jax.ShapeDtypeStruct((256, 128), BF),
            jax.ShapeDtypeStruct((64, 1024), F32),
        ),
        in_specs=[anywhere] * 7,
        out_specs=(vmem, vmem, vmem),
        scratch_shapes=[
            pltpu.VMEM((128, 1024), BF),
            pltpu.VMEM((256, 1024), BF),
            pltpu.VMEM((256, 1024), BF),
            pltpu.VMEM((128, 1024), BF),
            pltpu.VMEM((256, 128), BF),
            pltpu.VMEM((8, 256), jnp.int32),
            pltpu.VMEM((4, 32, 256), BF),
            pltpu.VMEM((Y, 2, 32, 1024), BF),
            pltpu.VMEM((F, 32, 1024), BF),
            pltpu.VMEM((4, 256, 1024), BF),
            pltpu.VMEM((2, F, 32, 512), F32),
            pltpu.VMEM((2, 2, 4, 2, 32, 512), BF),
            pltpu.VMEM((2, 2, 4, 2, 32, 512), BF),
            pltpu.VMEM((8, 32, 256), BF),
            pltpu.VMEM((8, 32, 256), BF),
            pltpu.VMEM((4, 32, 256), F32),
            pltpu.VMEM((Y, 2, 32, 1024), F32),
            pltpu.VMEM((4, 32, 1024), BF),
            pltpu.VMEM((4, 32, 1024), BF),
            pltpu.VMEM((8, 32, 1024), BF),
            pltpu.VMEM((8, 32, 1024), BF),
            pltpu.VMEM((3, 32, 1024), BF),
            pltpu.VMEM((3, 32, 1024), BF),
            dma((7,)), dma((16,)), dma((16,)), dma((26,)), dma((26,)), dma((12,)), dma((12,)),
            dma((32,)), dma((32,)), dma((8,)), dma((8,)), dma((4,)), dma((4,)), dma((8,)), dma((8,)), dma((3,)), dma((3,)),
        ],
        compiler_params=pltpu.CompilerParams(
            collective_id=0, has_side_effects=True, vmem_limit_bytes=48 * 1024 * 1024
        ),
    )(*held, jnp.broadcast_to(enc_lengths[:, None], (8, 256)))
    results = tuple(
        pltpu.with_memory_space_constraint(array, pltpu.VMEM) for array in (query_grad, encoder_grad, weight_grad)
    )
    query_grad, encoder_grad, weight_grad = pl.pallas_call(
        write_out,
        out_shape=tuple(jax.ShapeDtypeStruct(array.shape, array.dtype) for array in results),
        in_specs=[pl.BlockSpec(memory_space=pl.ANY)] * 3,
        out_specs=(pl.BlockSpec(memory_space=pltpu.HBM),) * 3,
        scratch_shapes=[dma((3,))],
    )(*results)
    return (query_grad[None], encoder_grad, weight_grad[None])


def solution(mesh):
    placed = (
        P("section", "dp", "mp"),
        P("section", "dp", "mp"),
        P("section", "dp", "mp"),
        P("section", "dp", "mp"),
        P("section", "dp", "mp"),
        P("dp", ("section", "mp")),
        P("dp"),
    )
    return jax.shard_map(
        shards,
        mesh=mesh,
        in_specs=placed,
        out_specs=(P("section", "dp", "mp"), P("dp", ("section", "mp")), P("section", "dp", "mp")),
        check_vma=False,
    )
```

```python
import jax
import jax.numpy as jnp
from jax import lax
from jax.experimental import pallas as pl
from jax.experimental.pallas import tpu as pltpu
from jax.sharding import PartitionSpec as P

HD = 256
NEG_FILL = -1e30
X, Z, Y = 4, 4, 8
F = X * Z
MESH = pl.DeviceIdType.MESH
BF = jnp.bfloat16
F32 = jnp.float32

NT = (((1,), (1,)), ((), ()))
NN = (((1,), (0,)), ((), ()))
TN = (((0,), (0,)), ((), ()))


def dot(a, b, dims):
    return lax.dot_general(a, b, dims, preferred_element_type=F32)


def kernel(
    q_hbm, k_hbm, v_hbm, d_hbm, w_hbm, enc_hbm, len_hbm,
    qg_ref, eg_ref, wg_ref,
    q_v, k_v, v_v, d_v, enc_v, len_v, et, ebuf, wbuf, kg,
    term, t_send, t_recv, l_send, l_recv, enc_sum,
    part, b_send, b_recv, z_send, z_recv,
    loc_sem, ws_sem, wr_sem, es_sem, er_sem, ks_sem, kr_sem,
    ts_sem, tr_sem, ls_sem, lr_sem, bs_sem, br_sem, zs_sem, zr_sem,
):
    dp = lax.axis_index("dp")
    y = lax.axis_index("section")
    m = lax.axis_index("mp")
    x = dp // 8
    z = (dp // 2) % 4
    c = dp % 2
    q = z % 2
    f = dp // 2

    def dev(x=x, z=z, c=c, y=y, m=m):
        return {"dp": x * 8 + z * 2 + c, "section": y, "mp": m}

    z_other = [z, z + 1 - 2 * q, (z + 2) % Z, Z - 1 - z]
    sister, m_other = 1 - c, 1 - m
    dev_x = [dev(x=(x + dx) % X) for dx in range(X)]
    dev_y = {step: dev(y=(y + Y + step) % Y) for step in (1, -1, 2, -2)}
    dev_z = [dev(z=other) for other in z_other]
    group = [dict(), dict(c=sister), dict(z=z_other[1]), dict(c=sister, z=z_other[1])]
    quarter = [c * 2 + q, sister * 2 + q, c * 2 + 1 - q, sister * 2 + 1 - q]
    dev_home = [dev(**other) for other in group]
    dev_away = [dev(m=m_other, **other) for other in group]

    loads = [
        pltpu.make_async_copy(src, dst, loc_sem.at[i])
        for i, (src, dst) in enumerate(
            [(enc_hbm, enc_v), (q_hbm, q_v), (k_hbm, k_v), (d_hbm, d_v), (v_hbm, v_v),
             (w_hbm.at[pl.ds(pl.multiple_of(q * 32, 32), 32)], wbuf.at[f]), (len_hbm, len_v)]
        )
    ]

    for copy in loads:
        copy.start()

    partners = dev_x[1:] + list(dev_y.values()) + dev_z[2:] + dev_home[1:] + dev_away
    barrier = pltpu.get_barrier_semaphore()
    for partner in partners:
        pl.semaphore_signal(barrier, inc=1, device_id=partner, device_id_type=MESH)
    loads[0].wait()
    et[...] = enc_v[...].astype(F32).T.astype(BF).reshape(4, 32, 256)
    ebuf[y, m, :, 0:256] = et[quarter[0]]
    pl.semaphore_wait(barrier, len(partners))

    sent = []

    def send(src, dst, ssem, rsem, device):
        copy = pltpu.make_async_remote_copy(
            src_ref=src, dst_ref=dst, send_sem=ssem, recv_sem=rsem, device_id=device, device_id_type=MESH
        )
        copy.start()
        sent.append(copy)
        return copy

    arrived = set()

    def arrive(inward, key):
        if (id(inward), key) not in arrived:
            arrived.add((id(inward), key))
            inward[key].wait_recv()

    e_in, w_in, k_in = {}, {}, {}

    def e_piece(across, j):
        number = 18 + across * 4 + j
        e_in[("piece", across, j)] = send(
            et.at[quarter[j]], ebuf.at[y, m, :, pl.ds(j * 256, 256)], es_sem.at[number], er_sem.at[number],
            dev_away[j] if across else dev_home[j],
        )

    def w_send(src, dst, dx, k, to):
        number = dx * 4 + k
        w_in[(dx, k)] = send(src, dst, ws_sem.at[number], wr_sem.at[number], to)

    def w_rows(half):
        return w_hbm.at[pl.ds(pl.multiple_of(half * 32, 32), 32)]

    def w_own():
        w_own_z()
        w_own_x()

    def w_own_z():
        for k in (1, 3, 2):
            w_send(w_rows(q if k == 2 else 1 - q), wbuf.at[f], 0, k, dev_z[k])

    def w_own_x():
        for dx in (1, 3, 2):
            w_send(w_rows(q), wbuf.at[f], X - dx, 0, dev_x[dx])

    def w_column(k):
        arrive(w_in, (0, k))
        slot = wbuf.at[x * Z + z_other[k]]
        for dx in (1, 3, 2):
            w_send(slot, slot, X - dx, k, dev_x[dx])

    def e_out(dm, dy, step, rows=None, number=None):
        slot = ebuf.at[(y + dy) % Y, m_other if dm else m]
        if rows is not None:
            slot = slot.at[pl.ds(rows, 16)]
        there = (dy - step) % Y
        if number is None:
            number = there
        e_in[(dm, number)] = send(
            slot, slot, es_sem.at[dm * 9 + number], er_sem.at[dm * 9 + number], dev_y[step]
        )

    def e_first(dm):
        for j in range(1 - dm, 4):
            arrive(e_in, ("piece", dm, j))
        e_out(dm, 0, 2)
        e_out(dm, 0, -2)

    def e_near(dm):
        e_out(dm, 0, 1)
        e_out(dm, 0, -1)

    def e_far(dm):
        arrive(e_in, (dm, 6))
        e_out(dm, 6, 2, 0, 4)
        e_out(dm, 6, 1)
        arrive(e_in, (dm, 2))
        e_out(dm, 2, -2, 16, 8)
        e_out(dm, 2, -1)

    def e_all(dm):
        for number in (1, 7, 2, 6, 3, 5, 4, 8):
            arrive(e_in, (dm, number))

    scale = HD ** (-0.5)

    def head(h):
        cols = slice(h * HD, (h + 1) * HD)
        qh, kh, vh, dh = q_v[:, cols], k_v[:, cols], v_v[:, cols], d_v[:, cols]
        scores = dot(qh, kh, NT) * scale
        scores = jnp.where(valid, scores, NEG_FILL)
        top = jnp.max(scores, axis=-1, keepdims=True)
        expo = jnp.exp(scores - top)
        probs = expo / jnp.sum(expo, axis=-1, keepdims=True)
        dprobs = dot(dh, vh, NT)
        delta = jnp.sum(probs * dprobs, axis=-1, keepdims=True)
        dscore = probs * (dprobs - delta) * scale
        kg[0, :, cols] = dot(dscore.T.astype(BF), qh, NN).astype(BF)
        k_send(2, h, 0, 2)
        k_send(1, h, 0, 1)
        qg_ref[:, cols] = dot(dscore.astype(BF), kh, NN).astype(BF)

    def k_send(j, h, src, to):
        cols = pl.ds(h * HD, HD)
        number = (j - 1) * 4 + h
        k_in[(j, h)] = send(
            kg.at[src, :, cols], kg.at[j, :, cols], ks_sem.at[number], kr_sem.at[number], dev_home[to]
        )

    def k_relay(h):
        arrive(k_in, (2, h))
        k_send(3, h, 2, 1)

    def eg_dot(t):
        grads = kg[2 * t : 2 * t + 2].reshape(512, 1024)
        term[t] = dot(wbuf[...].reshape(512, 1024), grads, NT).reshape(F, 32, 512)

    t_in = {}

    def t_out(t, up, k, half):
        yt = (y + k) % Y if up else (y + Y - k) % Y
        value = term[t, yt * 2 + half]
        if k < 3:
            arrive(t_in, (t, up, k + 1, half))
            value = value + t_recv[t, up, k, half].astype(F32)
        if k == 2 and half != up:
            arrive(t_in, (t, up, 4, half))
            value = value + t_recv[t, up, 3, half].astype(F32)
        t_send[t, up, k - 1, half] = value.astype(BF)
        number = ((t * 2 + up) * 4 + k - 1) * 2 + half
        step = 2 if k == 4 else 1
        t_in[(t, up, k, half)] = send(
            t_send.at[t, up, k - 1, half], t_recv.at[t, up, k - 1, half], ts_sem.at[number], tr_sem.at[number],
            dev_y[step if up else -step],
        )

    def eg_start(t):
        t_out(t, 1, 4, 0)
        t_out(t, 0, 4, 1)
        eg_step(t, 3)

    def eg_step(t, k):
        t_out(t, 1, k, 0)
        t_out(t, 0, k, 1)
        t_out(t, 1, k, 1)
        t_out(t, 0, k, 0)

    l_in = {}
    home = {}

    def l_out(across, j, value):
        number = across * 4 + j
        l_send[number] = value.astype(BF)
        l_in[(across, j)] = send(
            l_send.at[number], l_recv.at[number], ls_sem.at[number], lr_sem.at[number],
            dev_away[j] if across else dev_home[j],
        )

    def y_sum(t, half):
        return term[t, y * 2 + half] + t_recv[t, 1, 0, half].astype(F32) + t_recv[t, 0, 0, half].astype(F32)

    def eg_end(t):
        for up in (1, 0):
            for half in range(2):
                arrive(t_in, (t, up, 1, half))
        away = y_sum(t, m_other)
        l_out(1, 2 * t, away[:, 0:256])
        l_out(1, 2 * t + 1, away[:, 256:512])
        total = y_sum(t, m)
        if t == 0:
            home[0] = total[:, 0:256]
        else:
            l_out(0, 2, total[:, 0:256])
        l_out(0, 2 * t + 1, total[:, 256:512])

    first = (q + m) % 2

    def bit(turn):
        return 1 - first if turn else first

    def place(dx, turn, b):
        other = (z + 2 * b) % Z + bit(turn) * (1 - 2 * q)
        return ((x + dx) % X) * 2 + other // 2, other % 2

    def wg_dot(mt):
        rows = ebuf[:, mt].reshape(256, 1024)
        part[:, mt] = dot(rows, kg[...].reshape(1024, 1024), NN).reshape(Y, 32, 1024)

    b_in = {}

    def b_out(turn, b, dx):
        number = turn * 2 + b
        slot = (X - dx - 1) * 4 + number
        b_send[slot] = part[place(dx, turn, b)].astype(BF)
        b_in[(number, X - dx)] = send(
            b_send.at[slot], b_recv.at[slot], bs_sem.at[slot], br_sem.at[slot], dev_x[dx]
        )

    def wg_start(turn):
        for b in (1, 0):
            for dx in (2, 1, 3):
                b_out(turn, b, dx)

    def x_sum(turn, b, zt):
        value = part[x * 2 + zt // 2, zt % 2]
        for dx in (1, 2, 3):
            value = value + b_recv[(dx - 1) * 4 + turn * 2 + b].astype(F32)
        return value

    def z_copy(k):
        return pltpu.make_async_remote_copy(
            src_ref=z_send.at[k - 1], dst_ref=z_recv.at[k - 1], send_sem=zs_sem.at[k - 1], recv_sem=zr_sem.at[k - 1],
            device_id=dev_z[k], device_id_type=MESH,
        )

    def z_out(turn):
        for dx in (1, 3, 2):
            arrive(b_in, (turn * 2 + 1, dx))
        k = 2 + bit(turn)
        zt = (z + 2) % Z + bit(turn) * (1 - 2 * q)
        z_send[k - 1] = x_sum(turn, 1, zt).astype(BF)
        send(z_send.at[k - 1], z_recv.at[k - 1], zs_sem.at[k - 1], zr_sem.at[k - 1], dev(z=zt))

    def z_last():
        for turn in (0, 1):
            for dx in (1, 3, 2):
                arrive(b_in, (turn * 2, dx))
        z_send[0] = x_sum(1 - first, 0, z_other[1]).astype(BF)
        send(z_send.at[0], z_recv.at[0], zs_sem.at[0], zr_sem.at[0], dev_z[1])

    for j in (2, 3, 0, 1):
        e_piece(1, j)
    for j in (2, 3, 1):
        e_piece(0, j)
    w_own()
    for copy in loads[1:]:
        copy.wait()
    valid = lax.broadcasted_iota(jnp.int32, (128, 256), 1) < len_v[0:1, :]
    head(0)
    head(1)
    e_first(0)
    e_near(0)
    head(2)
    head(3)
    w_column(1)
    w_column(3)
    e_first(1)
    w_column(2)
    k_relay(0)
    e_far(0)
    e_near(1)
    k_relay(1)
    e_far(1)
    k_relay(2)
    for key in list(w_in):
        arrive(w_in, key)
    for h in range(4):
        arrive(k_in, (1, h))
    eg_dot(0)
    eg_start(0)
    k_relay(3)
    for key in list(k_in):
        arrive(k_in, key)
    eg_dot(1)
    eg_start(1)
    e_all(0)
    wg_dot(m)
    wg_start(0)
    eg_step(0, 2)
    e_all(1)
    wg_dot(m_other)
    wg_start(1)
    eg_step(1, 2)
    eg_step(0, 1)
    z_out(0)
    eg_step(1, 1)
    eg_end(0)
    eg_end(1)
    z_out(1)
    z_last()

    own = x_sum(first, 0, z)
    z_copy(2).wait_recv()
    wg_ref[pl.ds(pl.multiple_of(q * 32, 32), 32), :] = (own + z_recv[1].astype(F32)) * (1.0 / 32)
    z_copy(1).wait_recv()
    z_copy(3).wait_recv()
    wg_ref[pl.ds(pl.multiple_of((1 - q) * 32, 32), 32), :] = (
        z_recv[0].astype(F32) + z_recv[2].astype(F32)
    ) * (1.0 / 32)

    for key in list(l_in):
        arrive(l_in, key)
    for j in range(4):
        here = home[0] if j == 0 else l_recv[j].astype(F32)
        enc_sum[quarter[j]] = here + l_recv[4 + j].astype(F32)
    eg_ref[...] = enc_sum[...].reshape(128, 256).T.astype(BF)

    for copy in sent:
        copy.wait_send()


def write_out(a, b, c, a_out, b_out, c_out, sems):
    copies = [
        pltpu.make_async_copy(src, dst, sems.at[i])
        for i, (src, dst) in enumerate([(a, a_out), (b, b_out), (c, c_out)])
    ]
    for copy in copies:
        copy.start()
    for copy in copies:
        copy.wait()


def shards(queries, keys, values, out_grad, key_weight, encoded, enc_lengths):
    dma = pltpu.SemaphoreType.DMA
    anywhere = pl.BlockSpec(memory_space=pltpu.HBM)
    vmem = pl.BlockSpec(memory_space=pltpu.VMEM)
    held = [
        pltpu.with_memory_space_constraint(array, pltpu.HBM)
        for array in (queries[0], keys[0], values[0], out_grad[0], key_weight[0], encoded)
    ]
    query_grad, encoder_grad, weight_grad = pl.pallas_call(
        kernel,
        out_shape=(
            jax.ShapeDtypeStruct((128, 1024), BF),
            jax.ShapeDtypeStruct((256, 128), BF),
            jax.ShapeDtypeStruct((64, 1024), F32),
        ),
        in_specs=[anywhere] * 7,
        out_specs=(vmem, vmem, vmem),
        scratch_shapes=[
            pltpu.VMEM((128, 1024), BF),
            pltpu.VMEM((256, 1024), BF),
            pltpu.VMEM((256, 1024), BF),
            pltpu.VMEM((128, 1024), BF),
            pltpu.VMEM((256, 128), BF),
            pltpu.VMEM((8, 256), jnp.int32),
            pltpu.VMEM((4, 32, 256), BF),
            pltpu.VMEM((Y, 2, 32, 1024), BF),
            pltpu.VMEM((F, 32, 1024), BF),
            pltpu.VMEM((4, 256, 1024), BF),
            pltpu.VMEM((2, F, 32, 512), F32),
            pltpu.VMEM((2, 2, 4, 2, 32, 512), BF),
            pltpu.VMEM((2, 2, 4, 2, 32, 512), BF),
            pltpu.VMEM((8, 32, 256), BF),
            pltpu.VMEM((8, 32, 256), BF),
            pltpu.VMEM((4, 32, 256), F32),
            pltpu.VMEM((Y, 2, 32, 1024), F32),
            pltpu.VMEM((12, 32, 1024), BF),
            pltpu.VMEM((12, 32, 1024), BF),
            pltpu.VMEM((3, 32, 1024), BF),
            pltpu.VMEM((3, 32, 1024), BF),
            dma((7,)), dma((16,)), dma((16,)), dma((26,)), dma((26,)), dma((12,)), dma((12,)),
            dma((32,)), dma((32,)), dma((8,)), dma((8,)), dma((12,)), dma((12,)), dma((3,)), dma((3,)),
        ],
        compiler_params=pltpu.CompilerParams(
            collective_id=0, has_side_effects=True, vmem_limit_bytes=48 * 1024 * 1024
        ),
    )(*held, jnp.broadcast_to(enc_lengths[:, None], (8, 256)))
    results = tuple(
        pltpu.with_memory_space_constraint(array, pltpu.VMEM) for array in (query_grad, encoder_grad, weight_grad)
    )
    query_grad, encoder_grad, weight_grad = pl.pallas_call(
        write_out,
        out_shape=tuple(jax.ShapeDtypeStruct(array.shape, array.dtype) for array in results),
        in_specs=[pl.BlockSpec(memory_space=pl.ANY)] * 3,
        out_specs=(pl.BlockSpec(memory_space=pltpu.HBM),) * 3,
        scratch_shapes=[dma((3,))],
    )(*results)
    return (query_grad[None], encoder_grad, weight_grad[None])


def solution(mesh):
    placed = (
        P("section", "dp", "mp"),
        P("section", "dp", "mp"),
        P("section", "dp", "mp"),
        P("section", "dp", "mp"),
        P("section", "dp", "mp"),
        P("dp", ("section", "mp")),
        P("dp"),
    )
    return jax.shard_map(
        shards,
        mesh=mesh,
        in_specs=placed,
        out_specs=(P("section", "dp", "mp"), P("dp", ("section", "mp")), P("section", "dp", "mp")),
        check_vma=False,
    )
```

```python
import jax
import jax.numpy as jnp
from jax import lax
from jax.experimental import pallas as pl
from jax.experimental.pallas import tpu as pltpu
from jax.sharding import PartitionSpec as P

HD = 256
NEG_FILL = -1e30
X, Z, Y = 4, 4, 8
F = X * Z
MESH = pl.DeviceIdType.MESH
BF = jnp.bfloat16
F32 = jnp.float32

NT = (((1,), (1,)), ((), ()))
NN = (((1,), (0,)), ((), ()))
TN = (((0,), (0,)), ((), ()))


def dot(a, b, dims):
    return lax.dot_general(a, b, dims, preferred_element_type=F32)


def kernel(
    q_hbm, k_hbm, v_hbm, d_hbm, w_hbm, enc_hbm, len_hbm,
    qg_ref, eg_ref, wg_ref,
    q_v, k_v, v_v, d_v, enc_v, len_v, et, ebuf, wbuf, kg,
    term, t_send, t_recv, l_send, l_recv, enc_sum,
    part, b_send, b_recv, z_send, z_recv,
    loc_sem, ws_sem, wr_sem, es_sem, er_sem, ks_sem, kr_sem,
    ts_sem, tr_sem, ls_sem, lr_sem, bs_sem, br_sem, zs_sem, zr_sem,
):
    dp = lax.axis_index("dp")
    y = lax.axis_index("section")
    m = lax.axis_index("mp")
    x = dp // 8
    z = (dp // 2) % 4
    c = dp % 2
    q = z % 2
    f = dp // 2

    def dev(x=x, z=z, c=c, y=y, m=m):
        return {"dp": x * 8 + z * 2 + c, "section": y, "mp": m}

    z_other = [z, z + 1 - 2 * q, (z + 2) % Z, Z - 1 - z]
    sister, m_other = 1 - c, 1 - m
    dev_x = [dev(x=(x + dx) % X) for dx in range(X)]
    dev_y = {step: dev(y=(y + Y + step) % Y) for step in (1, -1, 2, -2)}
    dev_z = [dev(z=other) for other in z_other]
    group = [dict(), dict(c=sister), dict(z=z_other[1]), dict(c=sister, z=z_other[1])]
    quarter = [c * 2 + q, sister * 2 + q, c * 2 + 1 - q, sister * 2 + 1 - q]
    dev_home = [dev(**other) for other in group]
    dev_away = [dev(m=m_other, **other) for other in group]

    loads = [
        pltpu.make_async_copy(src, dst, loc_sem.at[i])
        for i, (src, dst) in enumerate(
            [(enc_hbm, enc_v), (q_hbm, q_v), (k_hbm, k_v), (d_hbm, d_v), (v_hbm, v_v),
             (w_hbm.at[pl.ds(pl.multiple_of(q * 32, 32), 32)], wbuf.at[f]), (len_hbm, len_v)]
        )
    ]

    for copy in loads:
        copy.start()

    partners = dev_x[1:] + list(dev_y.values()) + dev_z[2:] + dev_home[1:] + dev_away
    barrier = pltpu.get_barrier_semaphore()
    for partner in partners:
        pl.semaphore_signal(barrier, inc=1, device_id=partner, device_id_type=MESH)
    loads[0].wait()
    et[...] = enc_v[...].astype(F32).T.astype(BF).reshape(4, 32, 256)
    ebuf[y, m, :, 0:256] = et[quarter[0]]
    pl.semaphore_wait(barrier, len(partners))

    sent = []

    def send(src, dst, ssem, rsem, device):
        copy = pltpu.make_async_remote_copy(
            src_ref=src, dst_ref=dst, send_sem=ssem, recv_sem=rsem, device_id=device, device_id_type=MESH
        )
        copy.start()
        sent.append(copy)
        return copy

    arrived = set()

    def arrive(inward, key):
        if (id(inward), key) not in arrived:
            arrived.add((id(inward), key))
            inward[key].wait_recv()

    e_in, w_in, k_in = {}, {}, {}

    def e_piece(across, j):
        number = 18 + across * 4 + j
        e_in[("piece", across, j)] = send(
            et.at[quarter[j]], ebuf.at[y, m, :, pl.ds(j * 256, 256)], es_sem.at[number], er_sem.at[number],
            dev_away[j] if across else dev_home[j],
        )

    def w_send(src, dst, dx, k, to):
        number = dx * 4 + k
        w_in[(dx, k)] = send(src, dst, ws_sem.at[number], wr_sem.at[number], to)

    def w_rows(half):
        return w_hbm.at[pl.ds(pl.multiple_of(half * 32, 32), 32)]

    def w_own():
        w_own_z()
        w_own_x()

    def w_own_z():
        for k in (1, 3, 2):
            w_send(w_rows(q if k == 2 else 1 - q), wbuf.at[f], 0, k, dev_z[k])

    def w_own_x():
        for dx in (1, 3, 2):
            w_send(w_rows(q), wbuf.at[f], X - dx, 0, dev_x[dx])

    def w_column(k):
        arrive(w_in, (0, k))
        slot = wbuf.at[x * Z + z_other[k]]
        for dx in (1, 3, 2):
            w_send(slot, slot, X - dx, k, dev_x[dx])

    def e_out(dm, dy, step, rows=None, number=None):
        slot = ebuf.at[(y + dy) % Y, m_other if dm else m]
        if rows is not None:
            slot = slot.at[pl.ds(rows, 16)]
        there = (dy - step) % Y
        if number is None:
            number = there
        e_in[(dm, number)] = send(
            slot, slot, es_sem.at[dm * 9 + number], er_sem.at[dm * 9 + number], dev_y[step]
        )

    def e_first(dm):
        for j in range(1 - dm, 4):
            arrive(e_in, ("piece", dm, j))
        e_out(dm, 0, 2)
        e_out(dm, 0, -2)

    def e_near(dm):
        e_out(dm, 0, 1)
        e_out(dm, 0, -1)

    def e_far(dm):
        arrive(e_in, (dm, 6))
        e_out(dm, 6, 2, 0, 4)
        e_out(dm, 6, 1)
        arrive(e_in, (dm, 2))
        e_out(dm, 2, -2, 16, 8)
        e_out(dm, 2, -1)

    def e_all(dm):
        for number in (1, 7, 2, 6, 3, 5, 4, 8):
            arrive(e_in, (dm, number))

    scale = HD ** (-0.5)

    def head(h):
        cols = slice(h * HD, (h + 1) * HD)
        qh, kh, vh, dh = q_v[:, cols], k_v[:, cols], v_v[:, cols], d_v[:, cols]
        scores = dot(qh, kh, NT) * scale
        scores = jnp.where(valid, scores, NEG_FILL)
        top = jnp.max(scores, axis=-1, keepdims=True)
        expo = jnp.exp(scores - top)
        probs = expo / jnp.sum(expo, axis=-1, keepdims=True)
        dprobs = dot(dh, vh, NT)
        delta = jnp.sum(probs * dprobs, axis=-1, keepdims=True)
        dscore = probs * (dprobs - delta) * scale
        kg[0, :, cols] = dot(dscore.T.astype(BF), qh, NN).astype(BF)
        k_send(2, h, 0, 2)
        k_send(1, h, 0, 1)
        qg_ref[:, cols] = dot(dscore.astype(BF), kh, NN).astype(BF)

    def k_send(j, h, src, to):
        cols = pl.ds(h * HD, HD)
        number = (j - 1) * 4 + h
        k_in[(j, h)] = send(
            kg.at[src, :, cols], kg.at[j, :, cols], ks_sem.at[number], kr_sem.at[number], dev_home[to]
        )

    def k_relay(h):
        arrive(k_in, (2, h))
        k_send(3, h, 2, 1)

    def eg_dot(t):
        grads = kg[2 * t : 2 * t + 2].reshape(512, 1024)
        term[t] = dot(wbuf[...].reshape(512, 1024), grads, NT).reshape(F, 32, 512)

    t_in = {}

    def t_out(t, up, k, half):
        yt = (y + k) % Y if up else (y + Y - k) % Y
        value = term[t, yt * 2 + half]
        if k < 3:
            arrive(t_in, (t, up, k + 1, half))
            value = value + t_recv[t, up, k, half].astype(F32)
        if k == 2 and half != up:
            arrive(t_in, (t, up, 4, half))
            value = value + t_recv[t, up, 3, half].astype(F32)
        t_send[t, up, k - 1, half] = value.astype(BF)
        number = ((t * 2 + up) * 4 + k - 1) * 2 + half
        step = 2 if k == 4 else 1
        t_in[(t, up, k, half)] = send(
            t_send.at[t, up, k - 1, half], t_recv.at[t, up, k - 1, half], ts_sem.at[number], tr_sem.at[number],
            dev_y[step if up else -step],
        )

    def eg_start(t):
        t_out(t, 1, 4, 0)
        t_out(t, 0, 4, 1)
        eg_step(t, 3)

    def eg_step(t, k):
        t_out(t, 1, k, 0)
        t_out(t, 0, k, 1)
        t_out(t, 1, k, 1)
        t_out(t, 0, k, 0)

    l_in = {}
    home = {}

    def l_out(across, j, value):
        number = across * 4 + j
        l_send[number] = value.astype(BF)
        l_in[(across, j)] = send(
            l_send.at[number], l_recv.at[number], ls_sem.at[number], lr_sem.at[number],
            dev_away[j] if across else dev_home[j],
        )

    def y_sum(t, half):
        return term[t, y * 2 + half] + t_recv[t, 1, 0, half].astype(F32) + t_recv[t, 0, 0, half].astype(F32)

    def eg_end(t):
        for up in (1, 0):
            for half in range(2):
                arrive(t_in, (t, up, 1, half))
        away = y_sum(t, m_other)
        l_out(1, 2 * t, away[:, 0:256])
        l_out(1, 2 * t + 1, away[:, 256:512])
        total = y_sum(t, m)
        if t == 0:
            home[0] = total[:, 0:256]
        else:
            l_out(0, 2, total[:, 0:256])
        l_out(0, 2 * t + 1, total[:, 256:512])

    first = (q + m) % 2

    def bit(turn):
        return 1 - first if turn else first

    def place(dx, turn, b):
        other = (z + 2 * b) % Z + bit(turn) * (1 - 2 * q)
        return ((x + dx) % X) * 2 + other // 2, other % 2

    def wg_dot(mt):
        rows = ebuf[:, mt].reshape(256, 1024)
        part[:, mt] = dot(rows, kg[...].reshape(1024, 1024), NN).reshape(Y, 32, 1024)

    b_in = {}

    def b_out(turn, b, dx):
        number = turn * 2 + b
        slot = (X - dx - 1) * 4 + number
        b_send[slot] = part[place(dx, turn, b)].astype(BF)
        b_in[(number, X - dx)] = send(
            b_send.at[slot], b_recv.at[slot], bs_sem.at[slot], br_sem.at[slot], dev_x[dx]
        )

    def wg_start(turn):
        for b in (1, 0):
            for dx in (2, 1, 3):
                b_out(turn, b, dx)

    def x_sum(turn, b, zt):
        value = part[x * 2 + zt // 2, zt % 2]
        for dx in (1, 2, 3):
            value = value + b_recv[(dx - 1) * 4 + turn * 2 + b].astype(F32)
        return value

    def z_copy(k):
        return pltpu.make_async_remote_copy(
            src_ref=z_send.at[k - 1], dst_ref=z_recv.at[k - 1], send_sem=zs_sem.at[k - 1], recv_sem=zr_sem.at[k - 1],
            device_id=dev_z[k], device_id_type=MESH,
        )

    def z_out(turn):
        for dx in (1, 3, 2):
            arrive(b_in, (turn * 2 + 1, dx))
        k = 2 + bit(turn)
        zt = (z + 2) % Z + bit(turn) * (1 - 2 * q)
        z_send[k - 1] = x_sum(turn, 1, zt).astype(BF)
        send(z_send.at[k - 1], z_recv.at[k - 1], zs_sem.at[k - 1], zr_sem.at[k - 1], dev(z=zt))

    def z_last():
        for turn in (0, 1):
            for dx in (1, 3, 2):
                arrive(b_in, (turn * 2, dx))
        z_send[0] = x_sum(1 - first, 0, z_other[1]).astype(BF)
        send(z_send.at[0], z_recv.at[0], zs_sem.at[0], zr_sem.at[0], dev_z[1])

    for j in (2, 3, 0, 1):
        e_piece(1, j)
    for j in (2, 3, 1):
        e_piece(0, j)
    w_own()
    for copy in loads[1:]:
        copy.wait()
    valid = lax.broadcasted_iota(jnp.int32, (128, 256), 1) < len_v[0:1, :]
    head(0)
    head(1)
    e_first(0)
    e_near(0)
    head(2)
    head(3)
    w_column(1)
    w_column(3)
    e_first(1)
    w_column(2)
    k_relay(0)
    e_far(0)
    k_relay(1)
    e_near(1)
    e_far(1)
    k_relay(2)
    for key in list(w_in):
        arrive(w_in, key)
    for h in range(4):
        arrive(k_in, (1, h))
    eg_dot(0)
    eg_start(0)
    k_relay(3)
    for key in list(k_in):
        arrive(k_in, key)
    eg_dot(1)
    eg_start(1)
    e_all(0)
    wg_dot(m)
    wg_start(0)
    eg_step(0, 2)
    e_all(1)
    wg_dot(m_other)
    wg_start(1)
    eg_step(1, 2)
    eg_step(0, 1)
    z_out(0)
    eg_step(1, 1)
    eg_end(0)
    eg_end(1)
    z_out(1)
    z_last()

    own = x_sum(first, 0, z)
    z_copy(2).wait_recv()
    wg_ref[pl.ds(pl.multiple_of(q * 32, 32), 32), :] = (own + z_recv[1].astype(F32)) * (1.0 / 32)
    z_copy(1).wait_recv()
    z_copy(3).wait_recv()
    wg_ref[pl.ds(pl.multiple_of((1 - q) * 32, 32), 32), :] = (
        z_recv[0].astype(F32) + z_recv[2].astype(F32)
    ) * (1.0 / 32)

    for key in list(l_in):
        arrive(l_in, key)
    for j in range(4):
        here = home[0] if j == 0 else l_recv[j].astype(F32)
        enc_sum[quarter[j]] = here + l_recv[4 + j].astype(F32)
    eg_ref[...] = enc_sum[...].reshape(128, 256).T.astype(BF)

    for copy in sent:
        copy.wait_send()


def write_out(a, b, c, a_out, b_out, c_out, sems):
    copies = [
        pltpu.make_async_copy(src, dst, sems.at[i])
        for i, (src, dst) in enumerate([(a, a_out), (b, b_out), (c, c_out)])
    ]
    for copy in copies:
        copy.start()
    for copy in copies:
        copy.wait()


def shards(queries, keys, values, out_grad, key_weight, encoded, enc_lengths):
    dma = pltpu.SemaphoreType.DMA
    anywhere = pl.BlockSpec(memory_space=pltpu.HBM)
    vmem = pl.BlockSpec(memory_space=pltpu.VMEM)
    held = [
        pltpu.with_memory_space_constraint(array, pltpu.HBM)
        for array in (queries[0], keys[0], values[0], out_grad[0], key_weight[0], encoded)
    ]
    query_grad, encoder_grad, weight_grad = pl.pallas_call(
        kernel,
        out_shape=(
            jax.ShapeDtypeStruct((128, 1024), BF),
            jax.ShapeDtypeStruct((256, 128), BF),
            jax.ShapeDtypeStruct((64, 1024), F32),
        ),
        in_specs=[anywhere] * 7,
        out_specs=(vmem, vmem, vmem),
        scratch_shapes=[
            pltpu.VMEM((128, 1024), BF),
            pltpu.VMEM((256, 1024), BF),
            pltpu.VMEM((256, 1024), BF),
            pltpu.VMEM((128, 1024), BF),
            pltpu.VMEM((256, 128), BF),
            pltpu.VMEM((8, 256), jnp.int32),
            pltpu.VMEM((4, 32, 256), BF),
            pltpu.VMEM((Y, 2, 32, 1024), BF),
            pltpu.VMEM((F, 32, 1024), BF),
            pltpu.VMEM((4, 256, 1024), BF),
            pltpu.VMEM((2, F, 32, 512), F32),
            pltpu.VMEM((2, 2, 4, 2, 32, 512), BF),
            pltpu.VMEM((2, 2, 4, 2, 32, 512), BF),
            pltpu.VMEM((8, 32, 256), BF),
            pltpu.VMEM((8, 32, 256), BF),
            pltpu.VMEM((4, 32, 256), F32),
            pltpu.VMEM((Y, 2, 32, 1024), F32),
            pltpu.VMEM((12, 32, 1024), BF),
            pltpu.VMEM((12, 32, 1024), BF),
            pltpu.VMEM((3, 32, 1024), BF),
            pltpu.VMEM((3, 32, 1024), BF),
            dma((7,)), dma((16,)), dma((16,)), dma((26,)), dma((26,)), dma((12,)), dma((12,)),
            dma((32,)), dma((32,)), dma((8,)), dma((8,)), dma((12,)), dma((12,)), dma((3,)), dma((3,)),
        ],
        compiler_params=pltpu.CompilerParams(
            collective_id=0, has_side_effects=True, vmem_limit_bytes=48 * 1024 * 1024
        ),
    )(*held, jnp.broadcast_to(enc_lengths[:, None], (8, 256)))
    results = tuple(
        pltpu.with_memory_space_constraint(array, pltpu.VMEM) for array in (query_grad, encoder_grad, weight_grad)
    )
    query_grad, encoder_grad, weight_grad = pl.pallas_call(
        write_out,
        out_shape=tuple(jax.ShapeDtypeStruct(array.shape, array.dtype) for array in results),
        in_specs=[pl.BlockSpec(memory_space=pl.ANY)] * 3,
        out_specs=(pl.BlockSpec(memory_space=pltpu.HBM),) * 3,
        scratch_shapes=[dma((3,))],
    )(*results)
    return (query_grad[None], encoder_grad, weight_grad[None])


def solution(mesh):
    placed = (
        P("section", "dp", "mp"),
        P("section", "dp", "mp"),
        P("section", "dp", "mp"),
        P("section", "dp", "mp"),
        P("section", "dp", "mp"),
        P("dp", ("section", "mp")),
        P("dp"),
    )
    return jax.shard_map(
        shards,
        mesh=mesh,
        in_specs=placed,
        out_specs=(P("section", "dp", "mp"), P("dp", ("section", "mp")), P("section", "dp", "mp")),
        check_vma=False,
    )
```
